256 devices in a mesh: dp: 16 (over y_lo, x, core), shard: 16 (over z, y_hi).
Axes of the slice: x: 4, y: 4 (y_hi: 2, y_lo: 2; y = y_hi * 2 + y_lo), z: 8, core: 2. Of those that a mesh axis runs over, the one named last changes fastest.
Arguments:
- points: bfloat16 [32768, 256], P(('dp', 'shard')), may hold values from -48 to 48
- codebook: float32 [65536, 256], P('shard'), may hold values from -5 to 5
Outputs:
- updated: float32 [65536, 256], P('shard')
- log_partition: float32 [32768], P(('dp', 'shard'))
The draws below stay inside these ranges and needn't reach their ends.
All inputs are finite; a program needn't handle non-finite values.
Results may differ from the reference program's by a relative error of at most 0.0063.
Values may be sent and summed in bfloat16 or wider, within the bound.
A program may use at most 128 MiB of HBM per device.

```python
import math
import jax
import jax.numpy as jnp
from jax import lax

W = 256
K = 65536
TOTAL_ROWS = 32768


def shared_centers(key):
    return jnp.clip(jax.random.normal(jax.random.fold_in(key, 11), (K, W), jnp.float32), -5.0, 5.0)


def draw_codebook(key, part):
    centers = shared_centers(key)
    return centers


def draw_points(key, part):
    key = jax.random.fold_in(key, 5)
    keys = jax.random.split(key, 1)
    values = jax.random.normal(keys[0], (TOTAL_ROWS, W), jnp.float32)
    return jnp.clip(values, -48.0, 48.0).astype(jnp.bfloat16)


def setup_inputs(seed: int = 0) -> dict:
    key_list = jax.random.split(jax.random.key(seed), 3)
    return {
        "points": draw_points(jax.random.fold_in(key_list[2], 71), 0),
        "codebook": draw_codebook(jax.random.fold_in(key_list[2], 71), 0),
    }


def reference(points, codebook):
    sharpness = 4.0 / math.sqrt(W)
    narrow = codebook.astype(jnp.bfloat16)
    half_norm = 0.5 * lax.optimization_barrier(jnp.sum(codebook * codebook, axis=1))
    row_span = min(512, TOTAL_ROWS)
    blocked = points.reshape(TOTAL_ROWS // row_span, row_span, W)

    def advance(running, block_rows):
        centroid_sums, masses = running
        scores = sharpness * (lax.dot_general(block_rows, narrow, (((1,), (1,)), ((), ())), preferred_element_type=jnp.float32) - half_norm[None, :])
        row_peak = lax.optimization_barrier(jnp.max(scores, axis=1, keepdims=True))
        logsum = row_peak + jnp.log(lax.optimization_barrier(jnp.sum(jnp.exp(scores - row_peak), axis=1, keepdims=True)))
        assigned = jnp.exp(scores - logsum).astype(jnp.bfloat16)
        centroid_sums = centroid_sums + lax.dot_general(assigned, block_rows, (((0,), (0,)), ((), ())), preferred_element_type=jnp.float32)
        masses = masses + lax.optimization_barrier(jnp.sum(assigned.astype(jnp.float32), axis=0))
        return ((centroid_sums, masses), logsum[:, 0])
    start = (jnp.zeros((K, W), jnp.float32), jnp.zeros((K,), jnp.float32))
    (centroid_sums, masses), logsums = lax.scan(advance, start, blocked)
    updated = (centroid_sums + codebook) / (masses[:, None] + 1.0)
    return (updated, logsums.reshape(TOTAL_ROWS))
```

```python
import functools
import math

import jax
import jax.numpy as jnp
from jax import lax
from jax.experimental import pallas as pl
from jax.experimental.pallas import tpu as pltpu
from jax.sharding import PartitionSpec as P

MESH = pl.DeviceIdType.MESH
BF = jnp.bfloat16
F32 = jnp.float32
W = 256
K = 4096
RB = 128
GR = 2 * RB
R = 16 * RB
KC = 512
CH = 256
SHARP = 4.0 / math.sqrt(W)
C2 = SHARP / math.log(2.0)

NAMES = (
    ["p_y0", "p_z1", "p_z7", "p_z2", "p_z6", "p_z3", "p_z5", "p_z4a", "p_z4b", "p_q1", "p_q7"]
    + ["p_y2", "p_y6", "p_y3", "p_y5", "p_y4a", "p_y4b"]
    + [f"s_{a}{b}" for a in range(8) for b in range(2) if a or b]
    + [f"h_{a}{b}" for a in range(2) for b in range(4)]
    + [f"n_{a}{b}" for a in range(2) for b in range(4)]
    + ["r_12", "r_11", "r_13", "r_a", "r_b", "r_y", "r_p", "r_m"]
    + ["g_p", "g_m", "g_y", "g_a", "g_b", "g_11", "g_13", "g_ya", "g_yb"]
    + [f"t_{a}" for a in ("00", "01", "03", "10", "2a", "2b", "11", "13", "12a", "12b")]
)
INDEX = {name: i for i, name in enumerate(NAMES)}
ORDER = (0, 1, 7, 2, 6, 3, 5, 4)


def encode(value):
    return (value * jnp.abs(value)) * (value * value)


def decode(power):
    size = jnp.abs(power)
    root = lax.rsqrt(lax.rsqrt(jnp.maximum(size, 1e-37)))
    root = jnp.where(size < 1e-37, 0.0, root)
    return jnp.where(power < 0.0, -root, root)


def kernel(
    points, codebook, out, lse_out,
    cb, narrow, norm, pbuf, pf, fl, scores, ebuf, peaks, mine, stats, lse_abs, fpad, part, hpart, mpart, hmass,
    nmass, message, inbox, cb_sem, send_sem, recv_sem,
):
    dp, shard = lax.axis_index("dp"), lax.axis_index("shard")
    ylo, x, core = dp // 8, (dp // 2) % 4, dp % 2
    z, yhi = shard // 2, shard % 2

    def peer(dyl=0, dx=0, dc=0, dz=0, dyh=0):
        return {
            "dp": ((ylo + dyl) % 2) * 8 + ((x + dx + 4) % 4) * 2 + (core + dc) % 2,
            "shard": ((z + dz + 8) % 8) * 2 + (yhi + dyh) % 2,
        }

    barrier = pltpu.get_barrier_semaphore()
    others = [peer(dz=a, dyh=b) for a in range(8) for b in range(2) if a or b]
    others += [peer(dx=1), peer(dx=-1), peer(dyl=1), peer(dc=1)]
    for other in others:
        pl.semaphore_signal(barrier, inc=1, device_id=other, device_id_type=MESH)

    loads = []
    for i in range(4):
        rows = pl.ds(i * (K // 4), K // 4)
        loads.append(pltpu.make_async_copy(codebook.at[rows], cb.at[rows], cb_sem.at[i]))
        loads[-1].start()
    pbuf[0, 0:RB, :] = points[...]
    for i in range(4):
        loads[i].wait()

        def prepare(j, unused, i=i):
            rows = pl.ds(pl.multiple_of(i * (K // 4) + j * 256, 256), 256)
            value = cb[rows, :]
            narrow[rows, :] = value.astype(BF)
            half = 0.5 * jnp.sum(value * value, axis=1, keepdims=True)
            norm[rows, :] = jnp.broadcast_to(half, (256, 128))
            return unused

        lax.fori_loop(0, K // 4 // 256, prepare, 0)

    pl.semaphore_wait(barrier, len(others))

    sent = {}

    def copy(name, src, dst, device):
        i = INDEX[name]
        return pltpu.make_async_remote_copy(
            src_ref=src, dst_ref=dst, send_sem=send_sem.at[i], recv_sem=recv_sem.at[i],
            device_id=device, device_id_type=MESH,
        )

    def send(name, src, dst, device):
        sent[name] = copy(name, src, dst, device)
        sent[name].start()

    def await_(name, dst):
        copy(name, dst, dst, peer(dc=1)).wait_recv()

    def block(dz, dy, half=None):
        if half is None:
            return pbuf.at[dz % 8, pl.ds(dy * RB, RB)]
        return pbuf.at[dz % 8, pl.ds(dy * RB + half * (RB // 2), RB // 2)]

    own = block(0, 0)
    send("p_y0", own, block(0, 1), peer(dyh=1))
    send("p_z1", own, block(1, 0), peer(dz=-1))
    send("p_z7", own, block(7, 0), peer(dz=1))
    send("p_z2", own, block(2, 0), peer(dz=-2))
    send("p_z6", own, block(6, 0), peer(dz=2))

    def arrive(g):
        if g == 0:
            await_("p_y0", block(0, 1))
            send("p_q1", block(0, 1), block(1, 1), peer(dz=-1))
            send("p_q7", block(0, 1), block(7, 1), peer(dz=1))
        elif g == 1:
            await_("p_z1", block(1, 0))
            await_("p_z7", block(7, 0))
            await_("p_z2", block(2, 0))
            send("p_z3", block(2, 0), block(3, 0), peer(dz=-1))
            send("p_y2", block(2, 0), block(2, 1), peer(dyh=1))
            await_("p_z6", block(6, 0))
            send("p_z5", block(6, 0), block(5, 0), peer(dz=1))
            send("p_y6", block(6, 0), block(6, 1), peer(dyh=1))
            await_("p_q1", block(1, 1))
        elif g == 7:
            await_("p_q7", block(7, 1))
        elif g == 2:
            await_("p_z3", block(3, 0))
            send("p_z4a", block(3, 0, 0), block(4, 0, 0), peer(dz=-1))
            send("p_y3", block(3, 0), block(3, 1), peer(dyh=1))
            await_("p_z5", block(5, 0))
            send("p_z4b", block(5, 0, 1), block(4, 0, 1), peer(dz=1))
            send("p_y5", block(5, 0), block(5, 1), peer(dyh=1))
            await_("p_y2", block(2, 1))
        elif g == 6:
            await_("p_y6", block(6, 1))
        elif g == 3:
            await_("p_z4a", block(4, 0, 0))
            send("p_y4a", block(4, 0, 0), block(4, 1, 0), peer(dyh=1))
            await_("p_z4b", block(4, 0, 1))
            send("p_y4b", block(4, 0, 1), block(4, 1, 1), peer(dyh=1))
            await_("p_y3", block(3, 1))
        elif g == 5:
            await_("p_y5", block(5, 1))
        elif g == 4:
            await_("p_y4a", block(4, 1, 0))
            await_("p_y4b", block(4, 1, 1))

    def pass_one(g, slot, before, before_slot, before_peak):
        def body(i, carry):
            rows = pl.ds(pl.multiple_of(i * KC, KC), KC)
            peak, total = carry
            if g is not None:
                inner = lax.dot_general(
                    narrow[rows, :], pbuf[g], (((1,), (1,)), ((), ())), preferred_element_type=F32
                )
                half = norm[rows, :]
                inner = inner - jnp.concatenate([half, half], axis=1)
                scores[slot, rows, :] = inner
                peak = jnp.maximum(peak, jnp.max(inner.reshape(KC // 8, 8, GR), axis=0))
            if before is not None:
                shifted = scores[before_slot, rows, :].reshape(KC // 8, 8, GR) - before_peak[None]
                weight = jnp.exp2(shifted * C2)
                total = total + jnp.sum(weight, axis=0)
                ebuf[rows, before * GR : (before + 1) * GR] = weight.reshape(KC, GR).astype(BF)
            return peak, total

        start = (jnp.full((8, GR), -jnp.inf, F32), jnp.zeros((8, GR), F32))
        return lax.fori_loop(0, K // KC, body, start)

    before, before_peak = None, None
    for n, g in enumerate(ORDER + (None,)):
        if g is not None:
            arrive(g)
        peak, total = pass_one(g, n % 2, before, (n + 1) % 2, before_peak)
        if before is not None:
            row_peak = before_peak[0:1]
            row_lse = SHARP * row_peak + jnp.log(jnp.sum(total, axis=0, keepdims=True))
            plane = ((z + before) % 8) * 2
            peaks[2 * before : 2 * before + 1, :] = row_peak[:, 0:RB]
            peaks[2 * before + 1 : 2 * before + 2, :] = row_peak[:, RB:GR]
            mine[pl.ds(plane + yhi, 1), :] = row_lse[:, 0:RB]
            mine[pl.ds(plane + 1 - yhi, 1), :] = row_lse[:, RB:GR]
        if g is not None:
            before, before_peak = g, jnp.broadcast_to(jnp.max(peak, axis=0, keepdims=True), (8, GR))

    for a in range(8):
        for b in range(2):
            if a or b:
                send(f"s_{a}{b}", mine, stats.at[2 * a + b], peer(dz=a, dyh=b))
    stats[0] = mine[...]
    for a in range(8):
        for b in range(2):
            if a or b:
                await_(f"s_{a}{b}", stats.at[2 * a + b])
    every = stats[...]
    top = jnp.max(every, axis=0)
    lse_abs[...] = top + jnp.log(jnp.sum(jnp.exp(every - top[None]), axis=0))
    lse_out[...] = lse_abs[pl.ds(shard, 1), :]
    fpad[...] = jnp.zeros((128, 128), F32)
    for j in range(16):
        row = ((z + j // 2) % 8) * 2 + (yhi + j % 2) % 2
        fpad[j : j + 1, :] = jnp.exp(SHARP * peaks[j : j + 1, :] - lse_abs[pl.ds(row, 1), :])
    factor = fpad[...]
    column = jnp.transpose(factor)
    line = lax.broadcasted_iota(jnp.int32, (16, 128), 0)
    for j in range(16):
        rows = pbuf[j // 2, (j % 2) * RB : (j % 2 + 1) * RB, :].astype(F32)
        pf[j * RB : (j + 1) * RB, :] = (rows * column[:, j : j + 1]).astype(BF)
        value = jnp.broadcast_to(factor[j : j + 1, :], (16, 128))
        high = value.astype(BF).astype(F32)
        fl[:, j * RB : (j + 1) * RB] = jnp.where(
            line == 0, high, jnp.where(line == 1, value - high, 0.0)
        ).astype(BF)

    mine_at = pl.ds(pl.multiple_of(core * CH, CH), CH)
    sib_at = pl.ds(pl.multiple_of((1 - core) * CH, CH), CH)
    line2 = lax.broadcasted_iota(jnp.int32, (16, CH), 0)

    def first(dyl, dx):
        return (((ylo + dyl) % 2) * 4 + (x + dx) % 4) * (2 * CH)

    def weigh(dyl, dx):
        s = dyl * 4 + dx
        base = first(dyl, dx)
        part[s] = jnp.dot(
            ebuf[pl.ds(pl.multiple_of(base, 2 * CH), 2 * CH), :], pf[...], preferred_element_type=F32
        )
        for which, dst in ((core, mpart), (1 - core, hmass)):
            rows = pl.ds(pl.multiple_of(base + which * CH, CH), CH)
            mass = lax.dot_general(
                fl[...], ebuf[rows, :], (((1,), (1,)), ((), ())), preferred_element_type=F32
            )
            dst[s] = jnp.broadcast_to(mass[0:1] + mass[1:2], (8, CH))
        send(f"h_{dyl}{dx}", part.at[s, sib_at], hpart.at[s], peer(dc=1))
        send(f"n_{dyl}{dx}", hmass.at[s], nmass.at[s], peer(dc=1))

    def local(dyl, dx):
        s = dyl * 4 + dx
        await_(f"h_{dyl}{dx}", hpart.at[s])
        await_(f"n_{dyl}{dx}", nmass.at[s])
        return part[s, mine_at, :] + hpart[s], mpart[s, 0:1, :] + nmass[s, 0:1, :]

    def put(s, total, mass, split=False):
        high = mass.astype(BF).astype(F32)
        extra = jnp.where(line2 == 0, high, jnp.where(line2 == 1, mass - high, 0.0)).astype(BF)
        coded = encode(total).astype(BF)
        if split:
            message[s, 0:128, :] = coded[0:128]
            message[s, 128:144, :] = extra
            message[s, 144:272, :] = coded[128:256]
        else:
            message[s, 0:256, :] = coded
            message[s, 256:272, :] = extra

    def masses_in(rows):
        rows = rows.astype(F32)
        return rows[0:1] + rows[1:2]

    def got(name, s):
        await_(name, inbox.at[s])
        return decode(inbox[s, 0:256, :].astype(F32)), masses_in(inbox[s, 256:272, :])

    weigh(1, 2)
    weigh(1, 1)
    put(0, *local(1, 2))
    send("r_12", message.at[0], inbox.at[0], peer(dyl=1))
    weigh(1, 3)
    put(1, *local(1, 1))
    send("r_11", message.at[1], inbox.at[1], peer(dx=1))
    weigh(0, 2)
    put(2, *local(1, 3))
    send("r_13", message.at[2], inbox.at[2], peer(dx=-1))
    weigh(1, 0)
    total, mass = local(0, 2)
    other, other_mass = got("r_12", 0)
    put(3, total + other, mass + other_mass, split=True)
    send("r_a", message.at[3, pl.ds(0, 144)], inbox.at[3, pl.ds(0, 144)], peer(dx=1))
    send("r_b", message.at[3, pl.ds(144, 128)], inbox.at[3, pl.ds(144, 128)], peer(dx=-1))
    weigh(0, 1)
    total, mass = local(1, 0)
    for name, s in (("r_11", 1), ("r_13", 2)):
        other, other_mass = got(name, s)
        total, mass = total + other, mass + other_mass
    put(4, total, mass)
    send("r_y", message.at[4], inbox.at[4], peer(dyl=1))
    weigh(0, 3)
    weigh(0, 0)
    total, mass = local(0, 1)
    await_("r_a", inbox.at[3, pl.ds(0, 144)])
    total = jnp.concatenate([total[0:128] + decode(inbox[3, 0:128, :].astype(F32)), total[128:256]], axis=0)
    put(5, total, mass + masses_in(inbox[3, 128:144, :]))
    send("r_p", message.at[5], inbox.at[5], peer(dx=1))
    total, mass = local(0, 3)
    await_("r_b", inbox.at[3, pl.ds(144, 128)])
    total = jnp.concatenate([total[0:128], total[128:256] + decode(inbox[3, 144:272, :].astype(F32))], axis=0)
    put(6, total, mass)
    send("r_m", message.at[6], inbox.at[6], peer(dx=-1))
    total, mass = local(0, 0)
    for name, s in (("r_y", 4), ("r_p", 5), ("r_m", 6)):
        other, other_mass = got(name, s)
        total, mass = total + other, mass + other_mass

    def owned(dyl, dx, half=None, dc=0):
        start = first(dyl, dx) + ((core + dc) % 2) * CH
        if half is None:
            return out.at[pl.ds(pl.multiple_of(start, CH), CH)]
        return out.at[pl.ds(pl.multiple_of(start + half * (CH // 2), CH // 2), CH // 2)]

    own_at = pl.ds(pl.multiple_of(first(0, 0) + core * CH, CH), CH)
    wide = jnp.transpose(jnp.broadcast_to(mass, (128, CH))) + 1.0
    updated = (total + cb[own_at, :]) / jnp.concatenate([wide, wide], axis=1)
    out[own_at, :] = encode(updated).astype(BF)

    send("g_y", owned(0, 0), owned(0, 0), peer(dyl=1))
    send("g_p", owned(0, 0), owned(0, 0), peer(dx=1))
    send("g_m", owned(0, 0), owned(0, 0), peer(dx=-1))
    send("t_00", owned(0, 0), owned(0, 0), peer(dc=1))

    def relay(name, ref, sibling, *further):
        await_(name, ref)
        for target, device, piece in further:
            send(target, piece, piece, device)
        send(sibling, ref, ref, peer(dc=1))

    relay("g_y", owned(1, 0), "t_10", ("g_11", peer(dx=-1), owned(1, 0)), ("g_13", peer(dx=1), owned(1, 0)))
    relay("g_m", owned(0, 1), "t_01", ("g_a", peer(dx=-1), owned(0, 1, 0)))
    relay("g_p", owned(0, 3), "t_03", ("g_b", peer(dx=1), owned(0, 3, 1)))
    relay("g_a", owned(0, 2, 0), "t_2a", ("g_ya", peer(dyl=1), owned(0, 2, 0)))
    relay("g_b", owned(0, 2, 1), "t_2b", ("g_yb", peer(dyl=1), owned(0, 2, 1)))
    relay("g_11", owned(1, 1), "t_11")
    relay("g_13", owned(1, 3), "t_13")
    relay("g_ya", owned(1, 2, 0), "t_12a")
    relay("g_yb", owned(1, 2, 1), "t_12b")
    for name, ref in (
        ("t_00", owned(0, 0, dc=1)), ("t_10", owned(1, 0, dc=1)), ("t_01", owned(0, 1, dc=1)),
        ("t_03", owned(0, 3, dc=1)), ("t_2a", owned(0, 2, 0, dc=1)), ("t_2b", owned(0, 2, 1, dc=1)),
        ("t_11", owned(1, 1, dc=1)), ("t_13", owned(1, 3, dc=1)), ("t_12a", owned(1, 2, 0, dc=1)),
        ("t_12b", owned(1, 2, 1, dc=1)),
    ):
        await_(name, ref)
    for one in sent.values():
        one.wait_send()


def shards(points, codebook):
    n = len(NAMES)
    coded, lse = pl.pallas_call(
        kernel,
        out_shape=(jax.ShapeDtypeStruct((K, W), BF), jax.ShapeDtypeStruct((1, RB), F32)),
        in_specs=[pl.BlockSpec(memory_space=pltpu.VMEM), pl.BlockSpec(memory_space=pl.ANY)],
        out_specs=[pl.BlockSpec(memory_space=pltpu.VMEM)] * 2,
        scratch_shapes=[
            pltpu.VMEM((K, W), F32),
            pltpu.VMEM((K, W), BF),
            pltpu.VMEM((K, 128), F32),
            pltpu.VMEM((8, GR, W), BF),
            pltpu.VMEM((R, W), BF),
            pltpu.VMEM((16, R), BF),
            pltpu.VMEM((2, K, GR), F32),
            pltpu.VMEM((K, R), BF),
            pltpu.VMEM((16, RB), F32),
            pltpu.VMEM((16, RB), F32),
            pltpu.VMEM((16, 16, RB), F32),
            pltpu.VMEM((16, RB), F32),
            pltpu.VMEM((128, 128), F32),
            pltpu.VMEM((8, 2 * CH, W), F32),
            pltpu.VMEM((8, CH, W), F32),
            pltpu.VMEM((8, 8, CH), F32),
            pltpu.VMEM((8, 8, CH), F32),
            pltpu.VMEM((8, 8, CH), F32),
            pltpu.VMEM((7, CH + 16, W), BF),
            pltpu.VMEM((7, CH + 16, W), BF),
            pltpu.SemaphoreType.DMA((4,)),
            pltpu.SemaphoreType.DMA((n,)),
            pltpu.SemaphoreType.DMA((n,)),
        ],
        compiler_params=pltpu.CompilerParams(
            collective_id=0, has_side_effects=True, vmem_limit_bytes=60 << 20
        ),
        cost_estimate=pl.CostEstimate(flops=4 * R * K * W, bytes_accessed=8 << 20, transcendentals=R * K),
    )(points, codebook)
    return decode(coded.astype(F32)), lse.reshape(RB)


def solution(mesh):
    in_specs = (P(("dp", "shard"), None), P("shard", None))
    out_specs = (P("shard", None), P(("dp", "shard")))
    return jax.shard_map(shards, mesh=mesh, in_specs=in_specs, out_specs=out_specs, check_vma=False)
```

```python
import math

import jax
import jax.numpy as jnp
from jax import lax
from jax.experimental import pallas as pl
from jax.experimental.pallas import tpu as pltpu
from jax.sharding import PartitionSpec as P

MESH = pl.DeviceIdType.MESH
BF = jnp.bfloat16
F32 = jnp.float32
W = 256
K = 4096
RB = 128
GR = 2 * RB
R = 16 * RB
CH = 256
Q = 4
QR = CH // Q
SHARP = 4.0 / math.sqrt(W)
C2 = SHARP / math.log(2.0)

NAMES = (
    ["p_y0", "p_z1", "p_z7", "p_z2", "p_z6", "p_z3", "p_z5", "p_z4a", "p_z4b", "p_q1", "p_q7"]
    + ["p_y2", "p_y6", "p_y3", "p_y5", "p_y4a", "p_y4b"]
    + [f"s_{a}{b}" for a in range(8) for b in range(2) if a or b]
    + [f"h_{a}{b}" for a in range(2) for b in range(4)]
    + [f"n_{a}{b}" for a in range(2) for b in range(4)]
    + [f"r_{a}{q}" for a in ("12", "11", "13", "02", "y", "p", "m") for q in range(Q)]
    + [f"g_{a}{q}" for a in ("p", "m", "y", "2", "11", "13", "y2") for q in range(Q)]
    + [f"t_{a}{b}{q}" for a in range(2) for b in range(4) for q in range(Q)]
)
INDEX = {name: i for i, name in enumerate(NAMES)}
ORDER = (0, 1, 7, 2, 6, 3, 5, 4)


def encode(value):
    return (value * jnp.abs(value)) * (value * value)


def decode(power):
    size = jnp.abs(power)
    root = lax.rsqrt(lax.rsqrt(jnp.maximum(size, 1e-37)))
    root = jnp.where(size < 1e-37, 0.0, root)
    return jnp.where(power < 0.0, -root, root)


def kernel(
    points, codebook, out, lse_out,
    cb, narrow, norm, pbuf, pf, scores, ebuf, peaks, mine, stats, lse_abs, fpad, part, hpart, mpart,
    nmass, message, inbox, cb_sem, send_sem, recv_sem,
):
    dp, shard = lax.axis_index("dp"), lax.axis_index("shard")
    ylo, x, core = dp // 8, (dp // 2) % 4, dp % 2
    z, yhi = shard // 2, shard % 2

    def peer(dyl=0, dx=0, dc=0, dz=0, dyh=0):
        return {
            "dp": ((ylo + dyl) % 2) * 8 + ((x + dx + 4) % 4) * 2 + (core + dc) % 2,
            "shard": ((z + dz + 8) % 8) * 2 + (yhi + dyh) % 2,
        }

    barrier = pltpu.get_barrier_semaphore()
    others = [peer(dz=a) for a in (-2, -1, 1, 2)] + [peer(dyh=1)]
    others += [peer(dx=1), peer(dx=-1), peer(dyl=1), peer(dc=1)]
    for other in others:
        pl.semaphore_signal(barrier, inc=1, device_id=other, device_id_type=MESH)

    loads = []
    for i in range(4):
        rows = pl.ds(i * (K // 4), K // 4)
        loads.append(pltpu.make_async_copy(codebook.at[rows], cb.at[rows], cb_sem.at[i]))
        loads[-1].start()
    pbuf[0, 0:RB, :] = points[...]
    for i in range(4):
        loads[i].wait()

        def prepare(j, unused, i=i):
            rows = pl.ds(pl.multiple_of(i * (K // 4) + j * 256, 256), 256)
            value = cb[rows, :]
            narrow[rows, :] = value.astype(BF)
            half = 0.5 * jnp.sum(value * value, axis=1, keepdims=True)
            norm[rows, :] = jnp.broadcast_to(half, (256, 128))
            return unused

        lax.fori_loop(0, K // 4 // 256, prepare, 0)

    pl.semaphore_wait(barrier, len(others))

    sent = {}

    def copy(name, src, dst, device):
        i = INDEX[name]
        return pltpu.make_async_remote_copy(
            src_ref=src, dst_ref=dst, send_sem=send_sem.at[i], recv_sem=recv_sem.at[i],
            device_id=device, device_id_type=MESH,
        )

    def send(name, src, dst, device):
        sent[name] = copy(name, src, dst, device)
        sent[name].start()

    def await_(name, dst):
        copy(name, dst, dst, peer(dc=1)).wait_recv()

    def block(dz, dy, half=None):
        if half is None:
            return pbuf.at[dz % 8, pl.ds(dy * RB, RB)]
        return pbuf.at[dz % 8, pl.ds(dy * RB + half * (RB // 2), RB // 2)]

    own = block(0, 0)
    send("p_y0", own, block(0, 1), peer(dyh=1))
    send("p_z1", own, block(1, 0), peer(dz=-1))
    send("p_z7", own, block(7, 0), peer(dz=1))
    send("p_z2", own, block(2, 0), peer(dz=-2))
    send("p_z6", own, block(6, 0), peer(dz=2))

    def arrive(g):
        if g == 0:
            await_("p_y0", block(0, 1))
            send("p_q1", block(0, 1), block(1, 1), peer(dz=-1))
            send("p_q7", block(0, 1), block(7, 1), peer(dz=1))
        elif g == 1:
            await_("p_z1", block(1, 0))
            await_("p_z7", block(7, 0))
            await_("p_z2", block(2, 0))
            send("p_z3", block(2, 0), block(3, 0), peer(dz=-1))
            send("p_y2", block(2, 0), block(2, 1), peer(dyh=1))
            await_("p_z6", block(6, 0))
            send("p_z5", block(6, 0), block(5, 0), peer(dz=1))
            send("p_y6", block(6, 0), block(6, 1), peer(dyh=1))
            await_("p_q1", block(1, 1))
        elif g == 7:
            await_("p_q7", block(7, 1))
        elif g == 2:
            await_("p_z3", block(3, 0))
            send("p_z4a", block(3, 0, 0), block(4, 0, 0), peer(dz=-1))
            send("p_y3", block(3, 0), block(3, 1), peer(dyh=1))
            await_("p_z5", block(5, 0))
            send("p_z4b", block(5, 0, 1), block(4, 0, 1), peer(dz=1))
            send("p_y5", block(5, 0), block(5, 1), peer(dyh=1))
            await_("p_y2", block(2, 1))
        elif g == 6:
            await_("p_y6", block(6, 1))
        elif g == 3:
            await_("p_z4a", block(4, 0, 0))
            send("p_y4a", block(4, 0, 0), block(4, 1, 0), peer(dyh=1))
            await_("p_z4b", block(4, 0, 1))
            send("p_y4b", block(4, 0, 1), block(4, 1, 1), peer(dyh=1))
            await_("p_y3", block(3, 1))
        elif g == 5:
            await_("p_y5", block(5, 1))
        elif g == 4:
            await_("p_y4a", block(4, 1, 0))
            await_("p_y4b", block(4, 1, 1))

    def pass_one(g, slot, before, before_slot, before_peak):
        peak, total = jnp.full((8, GR), -jnp.inf, F32), None
        if g is not None:
            inner = lax.dot_general(
                narrow[...], pbuf[g], (((1,), (1,)), ((), ())), preferred_element_type=F32
            )
            half = norm[...]
            inner = inner - jnp.concatenate([half, half], axis=1)
            scores[slot] = inner
            peak = jnp.max(inner.reshape(K // 8, 8, GR), axis=0)
        if before is not None:
            shifted = scores[before_slot].reshape(K // 8, 8, GR) - before_peak[None]
            weight = jnp.exp2(shifted * C2)
            total = jnp.sum(weight, axis=0)
            ebuf[:, before * GR : (before + 1) * GR] = weight.reshape(K, GR).astype(BF)
        return peak, total

    before, before_peak = None, None
    for n, g in enumerate(ORDER + (None,)):
        if g is not None:
            arrive(g)
        peak, total = pass_one(g, n % 2, before, (n + 1) % 2, before_peak)
        if before is not None:
            row_peak = before_peak[0:1]
            row_lse = SHARP * row_peak + jnp.log(jnp.sum(total, axis=0, keepdims=True))
            plane = ((z + before) % 8) * 2
            peaks[2 * before : 2 * before + 1, :] = row_peak[:, 0:RB]
            peaks[2 * before + 1 : 2 * before + 2, :] = row_peak[:, RB:GR]
            mine[pl.ds(plane + yhi, 1), :] = row_lse[:, 0:RB]
            mine[pl.ds(plane + 1 - yhi, 1), :] = row_lse[:, RB:GR]
        if g is not None:
            before, before_peak = g, jnp.broadcast_to(jnp.max(peak, axis=0, keepdims=True), (8, GR))

    for a in range(8):
        for b in range(2):
            if a or b:
                send(f"s_{a}{b}", mine, stats.at[2 * a + b], peer(dz=a, dyh=b))
    stats[0] = mine[...]
    for a in range(8):
        for b in range(2):
            if a or b:
                await_(f"s_{a}{b}", stats.at[2 * a + b])
    every = stats[...]
    top = jnp.max(every, axis=0)
    lse_abs[...] = top + jnp.log(jnp.sum(jnp.exp(every - top[None]), axis=0))
    lse_out[...] = lse_abs[pl.ds(shard, 1), :]
    fpad[...] = jnp.zeros((128, 128), F32)
    for j in range(16):
        row = ((z + j // 2) % 8) * 2 + (yhi + j % 2) % 2
        fpad[j : j + 1, :] = jnp.exp(SHARP * peaks[j : j + 1, :] - lse_abs[pl.ds(row, 1), :])
    factor = fpad[...]
    column = jnp.transpose(factor)
    for j in range(16):
        rows = pbuf[j // 2, (j % 2) * RB : (j % 2 + 1) * RB, :].astype(F32)
        pf[j * RB : (j + 1) * RB, :] = (rows * column[:, j : j + 1]).astype(BF)

    mine_at = pl.ds(pl.multiple_of(core * CH, CH), CH)
    sib_at = pl.ds(pl.multiple_of((1 - core) * CH, CH), CH)
    line = lax.broadcasted_iota(jnp.int32, (16, CH), 0)

    def first(dyl, dx):
        return (((ylo + dyl) % 2) * 4 + (x + dx) % 4) * (2 * CH)

    def weigh(dyl, dx):
        s = dyl * 4 + dx
        rows = pl.ds(pl.multiple_of(first(dyl, dx), 2 * CH), 2 * CH)
        weights = ebuf[rows, :]
        part[s] = jnp.dot(weights, pf[...], preferred_element_type=F32)
        lanes = jnp.zeros((2 * CH, RB), F32)
        for j in range(16):
            lanes = lanes + weights[:, j * RB : (j + 1) * RB].astype(F32) * fpad[j : j + 1, :]
        for j in range(2 * CH // 128):
            mass = jnp.sum(jnp.transpose(lanes[j * 128 : (j + 1) * 128, :]), axis=0, keepdims=True)
            mpart[s, j // 2, :, (j % 2) * 128 : (j % 2 + 1) * 128] = jnp.broadcast_to(mass, (8, 128))
        send(f"h_{dyl}{dx}", part.at[s, sib_at], hpart.at[s], peer(dc=1))
        send(f"n_{dyl}{dx}", mpart.at[s, 1 - core], nmass.at[s], peer(dc=1))

    def local(dyl, dx):
        s = dyl * 4 + dx
        await_(f"h_{dyl}{dx}", hpart.at[s])
        await_(f"n_{dyl}{dx}", nmass.at[s])
        part[s, mine_at, :] = part[s, mine_at, :] + hpart[s]
        return mpart[s, core, 0:1, :] + nmass[s, 0:1, :]

    def piece(dyl, dx, q):
        return part[dyl * 4 + dx, pl.ds(pl.multiple_of(core * CH + q * QR, QR), QR), :]

    def slot(ref, s, q):
        return ref.at[s, pl.ds(0, 16 + QR)] if q == 0 else ref.at[s, pl.ds(16 + q * QR, QR)]

    def put(kind, s, q, total, mass, device):
        if q == 0:
            high = mass.astype(BF).astype(F32)
            message[s, 0:16, :] = jnp.where(
                line == 0, high, jnp.where(line == 1, mass - high, 0.0)
            ).astype(BF)
        message[s, 16 + q * QR : 16 + (q + 1) * QR, :] = encode(total).astype(BF)
        send(f"r_{kind}{q}", slot(message, s, q), slot(inbox, s, q), device)

    def got(kind, s, q):
        await_(f"r_{kind}{q}", slot(inbox, s, q))
        return decode(inbox[s, 16 + q * QR : 16 + (q + 1) * QR, :].astype(F32))

    def got_mass(s):
        rows = inbox[s, 0:16, :].astype(F32)
        return rows[0:1] + rows[1:2]

    weigh(1, 2)
    weigh(1, 1)
    mass = local(1, 2)
    for q in range(Q):
        put("12", 0, q, piece(1, 2, q), mass, peer(dyl=1))
    weigh(1, 3)
    mass = local(1, 1)
    for q in range(Q):
        put("11", 1, q, piece(1, 1, q), mass, peer(dx=1))
    weigh(0, 2)
    mass = local(1, 3)
    for q in range(Q):
        put("13", 2, q, piece(1, 3, q), mass, peer(dx=-1))
    weigh(0, 1)
    mass = local(0, 2)
    for q in (0, 2, 1, 3):
        total = piece(0, 2, q) + got("12", 0, q)
        if q == 0:
            mass = mass + got_mass(0)
        put("02", 3, q, total, mass, peer(dx=1 if q < Q // 2 else -1))
    weigh(0, 3)
    mass_p = local(0, 1)
    for q in range(Q // 2, Q):
        put("p", 5, q, piece(0, 1, q), mass_p, peer(dx=1))
    weigh(1, 0)
    mass_m = local(0, 3)
    for q in range(Q // 2):
        put("m", 6, q, piece(0, 3, q), mass_m, peer(dx=-1))
    weigh(0, 0)
    mass = local(1, 0)
    for q in range(Q):
        total = piece(1, 0, q) + got("11", 1, q) + got("13", 2, q)
        if q == 0:
            mass = mass + got_mass(1) + got_mass(2)
        put("y", 4, q, total, mass, peer(dyl=1))
        if q < Q // 2:
            total = piece(0, 1, q) + got("02", 3, q)
            if q == 0:
                mass_p = mass_p + got_mass(3)
            put("p", 5, q, total, mass_p, peer(dx=1))
            late = q + Q // 2
            put("m", 6, late, piece(0, 3, late) + got("02", 3, late), mass_m, peer(dx=-1))
    mass = local(0, 0)

    def owned(dyl, dx, q, dc=0):
        start = first(dyl, dx) + ((core + dc) % 2) * CH + q * QR
        return out.at[pl.ds(pl.multiple_of(start, QR), QR)]

    def spread(name, dyl, dx, q, *further):
        ref = owned(dyl, dx, q)
        if name is not None:
            await_(f"g_{name}{q}", ref)
        for target, device in further:
            send(f"g_{target}{q}", ref, ref, device)
        send(f"t_{dyl}{dx}{q}", ref, ref, peer(dc=1))

    wide = None
    for q in range(Q):
        total = piece(0, 0, q) + got("y", 4, q)
        if q < Q // 2:
            total = total + got("m", 6, q) + got("p", 5, q)
        else:
            total = total + got("p", 5, q) + got("m", 6, q)
        if q == 0:
            mass = mass + got_mass(4) + got_mass(5) + got_mass(6)
            wide = jnp.transpose(jnp.broadcast_to(mass, (128, CH))) + 1.0
        own_at = pl.ds(pl.multiple_of(first(0, 0) + core * CH + q * QR, QR), QR)
        below = wide[q * QR : (q + 1) * QR, :]
        updated = (total + cb[own_at, :]) / jnp.concatenate([below, below], axis=1)
        out[own_at, :] = encode(updated).astype(BF)
        spread(None, 0, 0, q, ("y", peer(dyl=1)), ("p", peer(dx=1)), ("m", peer(dx=-1)))
    for q in range(Q):
        spread("y", 1, 0, q, ("11", peer(dx=-1)), ("13", peer(dx=1)))
        spread("m", 0, 1, q, *([("2", peer(dx=-1))] if q < Q // 2 else []))
        spread("p", 0, 3, q, *([("2", peer(dx=1))] if q >= Q // 2 else []))
    for q in range(Q):
        spread("2", 0, 2, q, ("y2", peer(dyl=1)))
        spread("11", 1, 1, q)
        spread("13", 1, 3, q)
    for q in range(Q):
        spread("y2", 1, 2, q)
    for a in range(2):
        for b in range(4):
            for q in range(Q):
                await_(f"t_{a}{b}{q}", owned(a, b, q, dc=1))
    for one in sent.values():
        one.wait_send()


def decode_kernel(coded, updated):
    updated[...] = decode(coded[...].astype(F32))


def shards(points, codebook):
    n = len(NAMES)
    coded, lse = pl.pallas_call(
        kernel,
        out_shape=(jax.ShapeDtypeStruct((K, W), BF), jax.ShapeDtypeStruct((1, RB), F32)),
        in_specs=[pl.BlockSpec(memory_space=pltpu.VMEM), pl.BlockSpec(memory_space=pl.ANY)],
        out_specs=[pl.BlockSpec(memory_space=pltpu.VMEM)] * 2,
        scratch_shapes=[
            pltpu.VMEM((K, W), F32),
            pltpu.VMEM((K, W), BF),
            pltpu.VMEM((K, 128), F32),
            pltpu.VMEM((8, GR, W), BF),
            pltpu.VMEM((R, W), BF),
            pltpu.VMEM((2, K, GR), F32),
            pltpu.VMEM((K, R), BF),
            pltpu.VMEM((16, RB), F32),
            pltpu.VMEM((16, RB), F32),
            pltpu.VMEM((16, 16, RB), F32),
            pltpu.VMEM((16, RB), F32),
            pltpu.VMEM((128, 128), F32),
            pltpu.VMEM((8, 2 * CH, W), F32),
            pltpu.VMEM((8, CH, W), F32),
            pltpu.VMEM((8, 2, 8, CH), F32),
            pltpu.VMEM((8, 8, CH), F32),
            pltpu.VMEM((7, CH + 16, W), BF),
            pltpu.VMEM((7, CH + 16, W), BF),
            pltpu.SemaphoreType.DMA((4,)),
            pltpu.SemaphoreType.DMA((n,)),
            pltpu.SemaphoreType.DMA((n,)),
        ],
        compiler_params=pltpu.CompilerParams(
            collective_id=0, has_side_effects=True, vmem_limit_bytes=60 << 20
        ),
        cost_estimate=pl.CostEstimate(flops=4 * R * K * W, bytes_accessed=8 << 20, transcendentals=R * K),
    )(points, codebook)
    rows = K // 4
    updated = pl.pallas_call(
        decode_kernel,
        out_shape=jax.ShapeDtypeStruct((K, W), F32),
        grid=(4,),
        in_specs=[pl.BlockSpec((rows, W), lambda i: (i, 0))],
        out_specs=pl.BlockSpec((rows, W), lambda i: (i, 0)),
    )(coded)
    return updated, lse.reshape(RB)


def solution(mesh):
    in_specs = (P(("dp", "shard"), None), P("shard", None))
    out_specs = (P("shard", None), P(("dp", "shard")))
    return jax.shard_map(shards, mesh=mesh, in_specs=in_specs, out_specs=out_specs, check_vma=False)
```

```python
import math

import jax
import jax.numpy as jnp
from jax import lax
from jax.experimental import pallas as pl
from jax.experimental.pallas import tpu as pltpu
from jax.sharding import PartitionSpec as P

MESH = pl.DeviceIdType.MESH
BF = jnp.bfloat16
F32 = jnp.float32
W = 256
K = 4096
RB = 128
GR = 2 * RB
R = 16 * RB
CH = 256
Q = 2
QR = CH // Q
SHARP = 4.0 / math.sqrt(W)
C2 = SHARP / math.log(2.0)

NAMES = (
    ["p_y0", "p_z1", "p_z7", "p_z2", "p_z6", "p_z3", "p_z5", "p_z4a", "p_z4b", "p_q1", "p_q7"]
    + ["p_y2", "p_y6", "p_y3", "p_y5", "p_y4a", "p_y4b"]
    + [f"s_{a}{b}" for a in range(8) for b in range(2) if a or b]
    + [f"h_{a}{b}" for a in range(2) for b in range(4)]
    + [f"n_{a}{b}" for a in range(2) for b in range(4)]
    + [f"r_{a}{q}" for a in ("12", "11", "13", "02", "y", "p", "m") for q in range(Q)]
    + [f"g_{a}{q}" for a in ("p", "m", "y", "2", "11", "13", "y2") for q in range(Q)]
    + [f"t_{a}{b}{q}" for a in range(2) for b in range(4) for q in range(Q)]
)
INDEX = {name: i for i, name in enumerate(NAMES)}
ORDER = (0, 1, 7, 2, 6, 3, 5, 4)


def encode(value):
    return (value * jnp.abs(value)) * (value * value)


def decode(power):
    size = jnp.abs(power)
    root = lax.rsqrt(lax.rsqrt(jnp.maximum(size, 1e-37)))
    root = jnp.where(size < 1e-37, 0.0, root)
    return jnp.where(power < 0.0, -root, root)


def kernel(
    points, codebook, out, lse_out,
    cb, narrow, norm, pbuf, pf, scores, ebuf, peaks, mine, stats, lse_abs, fpad, part, hpart, mpart,
    nmass, message, inbox, cb_sem, send_sem, recv_sem,
):
    dp, shard = lax.axis_index("dp"), lax.axis_index("shard")
    ylo, x, core = dp // 8, (dp // 2) % 4, dp % 2
    z, yhi = shard // 2, shard % 2

    def peer(dyl=0, dx=0, dc=0, dz=0, dyh=0):
        return {
            "dp": ((ylo + dyl) % 2) * 8 + ((x + dx + 4) % 4) * 2 + (core + dc) % 2,
            "shard": ((z + dz + 8) % 8) * 2 + (yhi + dyh) % 2,
        }

    barrier = pltpu.get_barrier_semaphore()
    others = [peer(dz=a) for a in (-2, -1, 1, 2)] + [peer(dyh=1)]
    others += [peer(dx=1), peer(dx=-1), peer(dyl=1), peer(dc=1)]
    for other in others:
        pl.semaphore_signal(barrier, inc=1, device_id=other, device_id_type=MESH)

    loads = []
    for i in range(4):
        rows = pl.ds(i * (K // 4), K // 4)
        loads.append(pltpu.make_async_copy(codebook.at[rows], cb.at[rows], cb_sem.at[i]))
        loads[-1].start()
    pbuf[0, 0:RB, :] = points[...]
    for i in range(4):
        loads[i].wait()

        def prepare(j, unused, i=i):
            rows = pl.ds(pl.multiple_of(i * (K // 4) + j * 256, 256), 256)
            value = cb[rows, :]
            narrow[rows, :] = value.astype(BF)
            half = 0.5 * jnp.sum(value * value, axis=1, keepdims=True)
            norm[rows, :] = jnp.broadcast_to(half, (256, 128))
            return unused

        lax.fori_loop(0, K // 4 // 256, prepare, 0)

    pl.semaphore_wait(barrier, len(others))

    sent = {}

    def copy(name, src, dst, device):
        i = INDEX[name]
        return pltpu.make_async_remote_copy(
            src_ref=src, dst_ref=dst, send_sem=send_sem.at[i], recv_sem=recv_sem.at[i],
            device_id=device, device_id_type=MESH,
        )

    def send(name, src, dst, device):
        sent[name] = copy(name, src, dst, device)
        sent[name].start()

    def await_(name, dst):
        copy(name, dst, dst, peer(dc=1)).wait_recv()

    def block(dz, dy, half=None):
        if half is None:
            return pbuf.at[dz % 8, pl.ds(dy * RB, RB)]
        return pbuf.at[dz % 8, pl.ds(dy * RB + half * (RB // 2), RB // 2)]

    own = block(0, 0)
    send("p_y0", own, block(0, 1), peer(dyh=1))
    send("p_z1", own, block(1, 0), peer(dz=-1))
    send("p_z7", own, block(7, 0), peer(dz=1))
    send("p_z2", own, block(2, 0), peer(dz=-2))
    send("p_z6", own, block(6, 0), peer(dz=2))

    def arrive(g):
        if g == 0:
            await_("p_y0", block(0, 1))
            send("p_q1", block(0, 1), block(1, 1), peer(dz=-1))
            send("p_q7", block(0, 1), block(7, 1), peer(dz=1))
        elif g == 1:
            await_("p_z1", block(1, 0))
            await_("p_z7", block(7, 0))
            await_("p_z2", block(2, 0))
            send("p_z3", block(2, 0), block(3, 0), peer(dz=-1))
            send("p_y2", block(2, 0), block(2, 1), peer(dyh=1))
            await_("p_z6", block(6, 0))
            send("p_z5", block(6, 0), block(5, 0), peer(dz=1))
            send("p_y6", block(6, 0), block(6, 1), peer(dyh=1))
            await_("p_q1", block(1, 1))
        elif g == 7:
            await_("p_q7", block(7, 1))
        elif g == 2:
            await_("p_z3", block(3, 0))
            send("p_z4a", block(3, 0, 0), block(4, 0, 0), peer(dz=-1))
            send("p_y3", block(3, 0), block(3, 1), peer(dyh=1))
            await_("p_z5", block(5, 0))
            send("p_z4b", block(5, 0, 1), block(4, 0, 1), peer(dz=1))
            send("p_y5", block(5, 0), block(5, 1), peer(dyh=1))
            await_("p_y2", block(2, 1))
        elif g == 6:
            await_("p_y6", block(6, 1))
        elif g == 3:
            await_("p_z4a", block(4, 0, 0))
            send("p_y4a", block(4, 0, 0), block(4, 1, 0), peer(dyh=1))
            await_("p_z4b", block(4, 0, 1))
            send("p_y4b", block(4, 0, 1), block(4, 1, 1), peer(dyh=1))
            await_("p_y3", block(3, 1))
        elif g == 5:
            await_("p_y5", block(5, 1))
        elif g == 4:
            await_("p_y4a", block(4, 1, 0))
            await_("p_y4b", block(4, 1, 1))

    def pass_one(g, slot, before, before_slot, before_peak):
        peak, total = jnp.full((8, GR), -jnp.inf, F32), None
        if g is not None:
            inner = lax.dot_general(
                narrow[...], pbuf[g], (((1,), (1,)), ((), ())), preferred_element_type=F32
            )
            half = norm[...]
            inner = inner - jnp.concatenate([half, half], axis=1)
            scores[slot] = inner
            peak = jnp.max(inner.reshape(K // 8, 8, GR), axis=0)
        if before is not None:
            shifted = scores[before_slot].reshape(K // 8, 8, GR) - before_peak[None]
            weight = jnp.exp2(shifted * C2)
            total = jnp.sum(weight, axis=0)
            ebuf[:, before * GR : (before + 1) * GR] = weight.reshape(K, GR).astype(BF)
        return peak, total

    before, before_peak = None, None
    for n, g in enumerate(ORDER + (None,)):
        if g is not None:
            arrive(g)
        peak, total = pass_one(g, n % 2, before, (n + 1) % 2, before_peak)
        if before is not None:
            row_peak = before_peak[0:1]
            row_lse = SHARP * row_peak + jnp.log(jnp.sum(total, axis=0, keepdims=True))
            plane = ((z + before) % 8) * 2
            peaks[2 * before : 2 * before + 1, :] = row_peak[:, 0:RB]
            peaks[2 * before + 1 : 2 * before + 2, :] = row_peak[:, RB:GR]
            mine[pl.ds(plane + yhi, 1), :] = row_lse[:, 0:RB]
            mine[pl.ds(plane + 1 - yhi, 1), :] = row_lse[:, RB:GR]
        if g is not None:
            before, before_peak = g, jnp.broadcast_to(jnp.max(peak, axis=0, keepdims=True), (8, GR))

    for a in range(8):
        for b in range(2):
            if a or b:
                send(f"s_{a}{b}", mine, stats.at[2 * a + b], peer(dz=a, dyh=b))
    stats[0] = mine[...]
    for a in range(8):
        for b in range(2):
            if a or b:
                await_(f"s_{a}{b}", stats.at[2 * a + b])
    every = stats[...]
    top = jnp.max(every, axis=0)
    lse_abs[...] = top + jnp.log(jnp.sum(jnp.exp(every - top[None]), axis=0))
    lse_out[...] = lse_abs[pl.ds(shard, 1), :]
    fpad[...] = jnp.zeros((128, 128), F32)
    for j in range(16):
        row = ((z + j // 2) % 8) * 2 + (yhi + j % 2) % 2
        fpad[j : j + 1, :] = jnp.exp(SHARP * peaks[j : j + 1, :] - lse_abs[pl.ds(row, 1), :])
    factor = fpad[...]
    column = jnp.transpose(factor)
    for j in range(16):
        rows = pbuf[j // 2, (j % 2) * RB : (j % 2 + 1) * RB, :].astype(F32)
        pf[j * RB : (j + 1) * RB, :] = (rows * column[:, j : j + 1]).astype(BF)

    mine_at = pl.ds(pl.multiple_of(core * CH, CH), CH)
    sib_at = pl.ds(pl.multiple_of((1 - core) * CH, CH), CH)
    line = lax.broadcasted_iota(jnp.int32, (16, CH), 0)

    def first(dyl, dx):
        return (((ylo + dyl) % 2) * 4 + (x + dx) % 4) * (2 * CH)

    def weigh(dyl, dx):
        s = dyl * 4 + dx
        rows = pl.ds(pl.multiple_of(first(dyl, dx), 2 * CH), 2 * CH)
        weights = ebuf[rows, :]
        part[s] = jnp.dot(weights, pf[...], preferred_element_type=F32)
        lanes = jnp.zeros((2 * CH, RB), F32)
        for j in range(16):
            lanes = lanes + weights[:, j * RB : (j + 1) * RB].astype(F32) * fpad[j : j + 1, :]
        for j in range(2 * CH // 128):
            mass = jnp.sum(jnp.transpose(lanes[j * 128 : (j + 1) * 128, :]), axis=0, keepdims=True)
            mpart[s, j // 2, :, (j % 2) * 128 : (j % 2 + 1) * 128] = jnp.broadcast_to(mass, (8, 128))
        send(f"h_{dyl}{dx}", part.at[s, sib_at], hpart.at[s], peer(dc=1))
        send(f"n_{dyl}{dx}", mpart.at[s, 1 - core], nmass.at[s], peer(dc=1))

    def local(dyl, dx):
        s = dyl * 4 + dx
        await_(f"h_{dyl}{dx}", hpart.at[s])
        await_(f"n_{dyl}{dx}", nmass.at[s])
        part[s, mine_at, :] = part[s, mine_at, :] + hpart[s]
        return mpart[s, core, 0:1, :] + nmass[s, 0:1, :]

    def piece(dyl, dx, q):
        return part[dyl * 4 + dx, pl.ds(pl.multiple_of(core * CH + q * QR, QR), QR), :]

    def slot(ref, s, q):
        return ref.at[s, pl.ds(0, 16 + QR)] if q == 0 else ref.at[s, pl.ds(16 + q * QR, QR)]

    def put(kind, s, q, total, mass, device):
        if q == 0:
            high = mass.astype(BF).astype(F32)
            message[s, 0:16, :] = jnp.where(
                line == 0, high, jnp.where(line == 1, mass - high, 0.0)
            ).astype(BF)
        message[s, 16 + q * QR : 16 + (q + 1) * QR, :] = encode(total).astype(BF)
        send(f"r_{kind}{q}", slot(message, s, q), slot(inbox, s, q), device)

    def got(kind, s, q):
        await_(f"r_{kind}{q}", slot(inbox, s, q))
        return decode(inbox[s, 16 + q * QR : 16 + (q + 1) * QR, :].astype(F32))

    def got_mass(s):
        rows = inbox[s, 0:16, :].astype(F32)
        return rows[0:1] + rows[1:2]

    weigh(1, 2)
    weigh(1, 1)
    mass = local(1, 2)
    for q in range(Q):
        put("12", 0, q, piece(1, 2, q), mass, peer(dyl=1))
    weigh(1, 3)
    mass = local(1, 1)
    for q in range(Q):
        put("11", 1, q, piece(1, 1, q), mass, peer(dx=1))
    weigh(0, 2)
    mass = local(1, 3)
    for q in range(Q):
        put("13", 2, q, piece(1, 3, q), mass, peer(dx=-1))
    weigh(0, 1)
    mass = local(0, 2)
    for q in range(Q):
        total = piece(0, 2, q) + got("12", 0, q)
        if q == 0:
            mass = mass + got_mass(0)
        put("02", 3, q, total, mass, peer(dx=1 if q < Q // 2 else -1))
    weigh(0, 3)
    mass_p = local(0, 1)
    for q in range(Q // 2, Q):
        put("p", 5, q, piece(0, 1, q), mass_p, peer(dx=1))
    weigh(1, 0)
    mass_m = local(0, 3)
    for q in range(Q // 2):
        put("m", 6, q, piece(0, 3, q), mass_m, peer(dx=-1))
    weigh(0, 0)
    mass = local(1, 0)
    for q in range(Q):
        total = piece(1, 0, q) + got("11", 1, q) + got("13", 2, q)
        if q == 0:
            mass = mass + got_mass(1) + got_mass(2)
        put("y", 4, q, total, mass, peer(dyl=1))
        if q < Q // 2:
            total = piece(0, 1, q) + got("02", 3, q)
            if q == 0:
                mass_p = mass_p + got_mass(3)
            put("p", 5, q, total, mass_p, peer(dx=1))
            late = q + Q // 2
            put("m", 6, late, piece(0, 3, late) + got("02", 3, late), mass_m, peer(dx=-1))
    mass = local(0, 0)

    def owned(dyl, dx, q, dc=0):
        start = first(dyl, dx) + ((core + dc) % 2) * CH + q * QR
        return out.at[pl.ds(pl.multiple_of(start, QR), QR)]

    def spread(name, dyl, dx, q, *further):
        ref = owned(dyl, dx, q)
        if name is not None:
            await_(f"g_{name}{q}", ref)
        for target, device in further:
            send(f"g_{target}{q}", ref, ref, device)
        send(f"t_{dyl}{dx}{q}", ref, ref, peer(dc=1))

    wide = None
    for q in range(Q):
        total = piece(0, 0, q) + got("y", 4, q)
        if q < Q // 2:
            total = total + got("m", 6, q) + got("p", 5, q)
        else:
            total = total + got("p", 5, q) + got("m", 6, q)
        if q == 0:
            mass = mass + got_mass(4) + got_mass(5) + got_mass(6)
            wide = jnp.transpose(jnp.broadcast_to(mass, (128, CH))) + 1.0
        own_at = pl.ds(pl.multiple_of(first(0, 0) + core * CH + q * QR, QR), QR)
        below = wide[q * QR : (q + 1) * QR, :]
        updated = (total + cb[own_at, :]) / jnp.concatenate([below, below], axis=1)
        out[own_at, :] = encode(updated).astype(BF)
        spread(None, 0, 0, q, ("y", peer(dyl=1)), ("p", peer(dx=1)), ("m", peer(dx=-1)))
    for q in range(Q):
        spread("y", 1, 0, q, ("11", peer(dx=-1)), ("13", peer(dx=1)))
        spread("m", 0, 1, q, *([("2", peer(dx=-1))] if q < Q // 2 else []))
        spread("p", 0, 3, q, *([("2", peer(dx=1))] if q >= Q // 2 else []))
    for q in range(Q):
        spread("2", 0, 2, q, ("y2", peer(dyl=1)))
        spread("11", 1, 1, q)
        spread("13", 1, 3, q)
    for q in range(Q):
        spread("y2", 1, 2, q)
    for a in range(2):
        for b in range(4):
            for q in range(Q):
                await_(f"t_{a}{b}{q}", owned(a, b, q, dc=1))
    for one in sent.values():
        one.wait_send()


def decode_kernel(coded, updated):
    updated[...] = decode(coded[...].astype(F32))


def shards(points, codebook):
    n = len(NAMES)
    coded, lse = pl.pallas_call(
        kernel,
        out_shape=(jax.ShapeDtypeStruct((K, W), BF), jax.ShapeDtypeStruct((1, RB), F32)),
        in_specs=[pl.BlockSpec(memory_space=pltpu.VMEM), pl.BlockSpec(memory_space=pl.ANY)],
        out_specs=[pl.BlockSpec(memory_space=pltpu.VMEM)] * 2,
        scratch_shapes=[
            pltpu.VMEM((K, W), F32),
            pltpu.VMEM((K, W), BF),
            pltpu.VMEM((K, 128), F32),
            pltpu.VMEM((8, GR, W), BF),
            pltpu.VMEM((R, W), BF),
            pltpu.VMEM((2, K, GR), F32),
            pltpu.VMEM((K, R), BF),
            pltpu.VMEM((16, RB), F32),
            pltpu.VMEM((16, RB), F32),
            pltpu.VMEM((16, 16, RB), F32),
            pltpu.VMEM((16, RB), F32),
            pltpu.VMEM((128, 128), F32),
            pltpu.VMEM((8, 2 * CH, W), F32),
            pltpu.VMEM((8, CH, W), F32),
            pltpu.VMEM((8, 2, 8, CH), F32),
            pltpu.VMEM((8, 8, CH), F32),
            pltpu.VMEM((7, CH + 16, W), BF),
            pltpu.VMEM((7, CH + 16, W), BF),
            pltpu.SemaphoreType.DMA((4,)),
            pltpu.SemaphoreType.DMA((n,)),
            pltpu.SemaphoreType.DMA((n,)),
        ],
        compiler_params=pltpu.CompilerParams(
            collective_id=0, has_side_effects=True, vmem_limit_bytes=60 << 20
        ),
        cost_estimate=pl.CostEstimate(flops=4 * R * K * W, bytes_accessed=8 << 20, transcendentals=R * K),
    )(points, codebook)
    rows = K // 4
    updated = pl.pallas_call(
        decode_kernel,
        out_shape=jax.ShapeDtypeStruct((K, W), F32),
        grid=(4,),
        in_specs=[pl.BlockSpec((rows, W), lambda i: (i, 0))],
        out_specs=pl.BlockSpec((rows, W), lambda i: (i, 0)),
    )(coded)
    return updated, lse.reshape(RB)


def solution(mesh):
    in_specs = (P(("dp", "shard"), None), P("shard", None))
    out_specs = (P("shard", None), P(("dp", "shard")))
    return jax.shard_map(shards, mesh=mesh, in_specs=in_specs, out_specs=out_specs, check_vma=False)
```
